512 devices in a mesh: queue: 64 (over x, y, z_hi, core), head: 8 (over z_lo).
Axes of the slice: x: 4, y: 4, z: 16 (z_hi: 2, z_lo: 8; z = z_hi * 8 + z_lo), core: 2. Of those that a mesh axis runs over, the one named last changes fastest.
Arguments:
- projected: bfloat16 [32768, 3, 3072], P(('queue', 'head')), may hold values from -24 to 24
- prompt_states: bfloat16 [8, 2, 128, 3072], P(None, None, None, 'head'), may hold values from -24 to 24
- region_map: int32 [64, 512], P('queue'), may hold values from 0 to 3
- region_prompt: int32 [64, 4], P('queue'), may hold values from 0 to 7
- step_index: int32 [64], P('queue'), may hold values from 0 to 49
- time_gates: float32 [50, 3072], P(None, 'head'), may hold values from 0.1 to 1.9
- incoming: bfloat16 [512, 3072], P('head'), may hold values from -4 to 4
Outputs:
- advanced: bfloat16 [32768, 3072], P(('queue', 'head'))
The draws below stay inside these ranges and needn't reach their ends.
All inputs are finite; a program needn't handle non-finite values.
Results may differ from the reference program's by a relative error of at most 0.003.
Values may be sent and summed in bfloat16 or wider, within the bound.
A program may use at most 64 MiB of HBM per device.

```python
import math
import jax
import jax.numpy as jnp
from jax import lax

HD = 128
HEADS = 24
P_SIZE = 512
L = 128
R = 4
NPROMPT = 8
NSTEPS = 50
C = 3072
NQ = 64
TOKENS = 32768


def draw_projected(key, part):
    key = jax.random.fold_in(key, 11)
    scales = jnp.array([2.5, 1.0, 1.0], jnp.float32)[None, :, None]
    base = jnp.clip(jax.random.normal(key, (TOKENS, 3, C), jnp.float32) * scales, -24.0, 24.0)
    return base.astype(jnp.bfloat16)


def draw_prompt_states(key, part):
    key = jax.random.fold_in(key, 23)
    base = jnp.clip(jax.random.normal(key, (NPROMPT, 2, L, C), jnp.float32), -24.0, 24.0)
    return base.astype(jnp.bfloat16)


def with_ends(values, rng, low, largest):
    longest = values.shape.index(max(values.shape))
    spots = []
    for shift in (0, 1):
        where = [jax.random.randint(jax.random.fold_in(rng, axis), (), 0, length) for axis, length in enumerate(values.shape)]
        where[longest] = (where[longest] + shift) % values.shape[longest]
        spots.append(tuple(where))
    return values.at[spots[0]].set(low).at[spots[1]].set(largest)


def steps_of(stream_key, shape, pieces, smallest, top_value):
    level = 1.0
    for axis_at, parts in pieces:
        draws = jax.random.uniform(jax.random.fold_in(jax.random.fold_in(stream_key, 6), axis_at), (parts,), jnp.float32, smallest / len(pieces), top_value / len(pieces))
        level = level * jnp.repeat(jnp.exp(draws), shape[axis_at] // parts).reshape((-1,) + (1,) * (len(shape) - 1 - axis_at))
    return level


def bell_draw(key, dims, deviation, limit, split=(), held_as=jnp.bfloat16):
    values = deviation * jax.random.normal(key, dims, jnp.float32)
    if split:
        values = values * steps_of(key, dims, split, -0.22, 0.18)
    return jnp.clip(values, -limit, limit).astype(held_as)


def setup_inputs(seed: int = 0) -> dict:
    keys = jax.random.split(jax.random.key(seed), 8)
    return {
        "projected": draw_projected(jax.random.fold_in(keys[7], 71), 0),
        "prompt_states": draw_prompt_states(jax.random.fold_in(keys[7], 71), 0),
        "region_map": with_ends(jax.random.randint(keys[2], (NQ, P_SIZE), 0, R), jax.random.fold_in(keys[2], 1), 0, R - 1).astype(jnp.int32),
        "region_prompt": with_ends(jax.random.randint(keys[3], (NQ, R), 0, NPROMPT), jax.random.fold_in(keys[3], 1), 0, NPROMPT - 1).astype(jnp.int32),
        "step_index": with_ends(jax.random.randint(keys[4], (NQ,), 0, NSTEPS), jax.random.fold_in(keys[4], 1), 0, NSTEPS - 1).astype(jnp.int32),
        "time_gates": jnp.clip(1.0 + 0.18 * jax.random.normal(keys[5], (NSTEPS, C), jnp.float32), 0.1, 1.9),
        "incoming": bell_draw(keys[6], (P_SIZE, C), 0.5, 4.0, ((0, 8),)),
    }


NEG = -1e+30

def attend(queries, key_rows, value_rows, allowed):
    scores = jnp.dot(queries, key_rows.T, preferred_element_type=jnp.float32) * (1.0 / math.sqrt(HD))
    scores = jnp.where(allowed, scores, NEG)
    highest = lax.optimization_barrier(jnp.max(scores, axis=1, keepdims=True))
    weights = jnp.exp(scores - highest)
    totals = lax.optimization_barrier(jnp.sum(weights, axis=1, keepdims=True))
    rounded = weights.astype(jnp.bfloat16)
    return jnp.dot(rounded, value_rows, preferred_element_type=jnp.float32) / totals

def reference(projected, prompt_states, region_map, region_prompt, step_index, time_gates, incoming):
    slabs = projected.reshape(NQ, P_SIZE, 3, HEADS, HD)
    padded = jnp.pad(slabs[:, :, 1:3], ((1, 1), (0, 0), (0, 0), (0, 0), (0, 0)))
    key_region = jnp.arange(R * L, dtype=jnp.int32) // L

    def one_slab(index):
        own = lax.dynamic_index_in_dim(slabs, index, 0, keepdims=False)
        window = lax.dynamic_slice_in_dim(padded, index, 3, 0).reshape(3 * P_SIZE, 2, HEADS, HD)
        present = jnp.arange(3, dtype=jnp.int32) + index - 1
        valid = (present >= 0) & (present < NQ)
        allowed_self = jnp.broadcast_to(jnp.repeat(valid, P_SIZE)[None, :], (P_SIZE, 3 * P_SIZE))
        prompts_here = lax.dynamic_index_in_dim(region_prompt, index, 0, keepdims=False)
        chosen = prompt_states[prompts_here]
        chosen = chosen.transpose(1, 0, 2, 3).reshape(2, R * L, HEADS, HD)
        regions_here = lax.dynamic_index_in_dim(region_map, index, 0, keepdims=False)
        allowed_cross = regions_here[:, None] == key_region[None, :]
        inputs = (own[:, 0].transpose(1, 0, 2), window[:, 0].transpose(1, 0, 2), window[:, 1].transpose(1, 0, 2), chosen[0].transpose(1, 0, 2), chosen[1].transpose(1, 0, 2))

        def one_head(items):
            self_out = attend(items[0], items[1], items[2], allowed_self)
            cross_out = attend(items[0], items[3], items[4], allowed_cross)
            return self_out + cross_out
        summed = lax.map(one_head, inputs).transpose(1, 0, 2).reshape(P_SIZE, C)
        step_here = lax.dynamic_index_in_dim(step_index, index, 0, keepdims=False)
        gate_row = lax.dynamic_index_in_dim(time_gates, step_here, 0, keepdims=False)
        return (gate_row[None, :] * summed).astype(jnp.bfloat16)
    results = lax.map(one_slab, jnp.arange(NQ, dtype=jnp.int32))
    advanced = jnp.concatenate([incoming[None], results[:-1]], axis=0)
    return advanced.reshape(NQ * P_SIZE, C)
```

```python
import math

import jax
import jax.numpy as jnp
from jax import lax
from jax.experimental import pallas as pl
from jax.experimental.pallas import tpu as pltpu
from jax.sharding import PartitionSpec as P

HD = 128
L = 128
R = 4
NPROMPT = 8
GROUP = 4
PER = 3

NEG = -1e30
FAR = 1e30
SCALE = math.log2(math.e) / math.sqrt(HD)
MESH = pl.DeviceIdType.MESH


def worker_of(z, hl):
    free = lax.rem(z, 2) * 2 + 1
    return hl + jnp.where(hl >= free, 1, 0)


def attention_kernel(
    nq, nz,
    proj, prompts, rmap, rprompt, step, gates,
    out,
    kv, qb, ob, pkv, rmap_v, gates_v, meta_src, meta,
    kv_sem, q_sem, halo_sem, meta_sem, out_sem, local_sem,
    send_sem, halo_send, meta_send, out_send,
):
    rows = proj.shape[1]
    slab = rows * nz
    half = slab // 2
    heads = PER * nz
    q = lax.axis_index("queue")
    j = lax.axis_index("head")
    c = lax.div(q, GROUP)
    a = lax.rem(q, GROUP)
    free = lax.rem(j, 2) * 2 + 1
    works = a != free
    hl = a - jnp.where(a > free, 1, 0)
    right = lax.rem(q + GROUP, nq)
    left = lax.rem(q + nq - GROUP, nq)
    place = a * nz + j
    members = GROUP * nz

    barrier = pltpu.get_barrier_semaphore()

    def greet(i, carry):
        other = lax.rem(place + i, members)
        pl.semaphore_signal(
            barrier, inc=1,
            device_id={"queue": c * GROUP + lax.div(other, nz), "head": lax.rem(other, nz)},
            device_id_type=MESH,
        )
        return carry

    lax.fori_loop(1, members, greet, 0)
    for side in (left, right):
        pl.semaphore_signal(
            barrier, inc=1, device_id={"queue": side, "head": j}, device_id_type=MESH
        )
    map_copy = pltpu.make_async_copy(rmap, rmap_v, local_sem.at[0])
    gate_copy = pltpu.make_async_copy(gates, gates_v, local_sem.at[1])
    lane = pl.multiple_of(jnp.minimum(hl, PER - 1) * HD, HD)
    prompt_copy = pltpu.make_async_copy(
        prompts.at[:, :, :, pl.ds(lane, HD)], pkv, local_sem.at[2]
    )
    map_copy.start()
    gate_copy.start()
    prompt_copy.start()
    pl.semaphore_wait(barrier, members + 1)

    def spread(first, last, dst, sem):
        def body(n, carry):
            z2 = lax.rem(j + lax.div(n, PER), nz)
            hl2 = lax.rem(n, PER)
            a2 = worker_of(z2, hl2)
            col = pl.multiple_of((z2 * PER + hl2) * HD, HD)
            src = proj.at[first:last, :, pl.ds(col, HD)]
            mine = (a2 == a) & (z2 == j)

            @pl.when(mine)
            def _():
                pltpu.make_async_copy(src, dst, sem).start()

            @pl.when(jnp.logical_not(mine))
            def _():
                pltpu.make_async_remote_copy(
                    src_ref=src, dst_ref=dst, send_sem=send_sem, recv_sem=sem,
                    device_id={"queue": c * GROUP + a2, "head": z2}, device_id_type=MESH,
                ).start()

            return carry

        lax.fori_loop(0, heads, body, 0)

    kv_row = pl.multiple_of((a + 1) * slab + j * rows, rows)
    spread(1, 3, kv.at[:, pl.ds(kv_row, rows), :], kv_sem.at[a])

    map_copy.wait()
    gate_copy.wait()
    regions = rmap_v[...]
    token_prompt = jnp.zeros(regions.shape, jnp.int32)
    for r in range(R):
        token_prompt = jnp.where(regions == r, rprompt[0, r], token_prompt)
    token_prompt = token_prompt.astype(jnp.float32)
    for i in range(slab // 128):
        meta_src[i : i + 1, :] = token_prompt[:, i * 128 : (i + 1) * 128]
    table = gates_v[...]
    picked = lax.broadcasted_iota(jnp.int32, table.shape, 0) == step[0]
    gate_row = jnp.sum(jnp.where(picked, table, 0.0), axis=0, keepdims=True)
    for i in range(PER):
        meta_src[4 + i : 5 + i, :] = gate_row[:, i * HD : (i + 1) * HD]
    meta_src[7:8, :] = jnp.zeros((1, 128), jnp.float32)
    pltpu.make_async_copy(meta_src, meta.at[a], meta_sem).start()
    for i in range(1, GROUP):
        pltpu.make_async_remote_copy(
            src_ref=meta_src, dst_ref=meta.at[a], send_sem=meta_send.at[i - 1], recv_sem=meta_sem,
            device_id={"queue": c * GROUP + lax.rem(a + i, GROUP), "head": j},
            device_id_type=MESH,
        ).start()

    q_row = pl.multiple_of(a * slab + j * rows, rows)
    part = lax.div(j, nz // 2)
    spread(0, 1, qb.at[:, pl.ds(q_row, rows), :], q_sem.at[a * 2 + part])

    def wait_for(ref, sem):
        pltpu.make_async_copy(ref, ref, sem).wait()

    wait_for(meta, meta_sem)
    prompt_copy.wait()

    @pl.when(works)
    def _():
        for s in range(GROUP):
            wait_for(kv.at[:, (s + 1) * slab : (s + 2) * slab, :], kv_sem.at[s])
        halos = (
            (1, GROUP + 1, left, 0),
            (GROUP, 0, right, 1),
        )
        copies = [
            pltpu.make_async_remote_copy(
                src_ref=kv.at[:, src * slab : (src + 1) * slab, :],
                dst_ref=kv.at[:, dst * slab : (dst + 1) * slab, :],
                send_sem=halo_send.at[k], recv_sem=halo_sem.at[k],
                device_id={"queue": side, "head": j}, device_id_type=MESH,
            )
            for src, dst, side, k in halos
        ]
        for copy in copies:
            copy.start()
        head_col = pl.multiple_of((j * PER + hl) * HD, HD)
        pk = [pkv.at[p, 0] for p in range(NPROMPT)]
        ones = jnp.ones((3 * slab, HD), jnp.bfloat16)

        def one_slab(t, carry):
            s = lax.rem(t + 1, GROUP)

            @pl.when(t == 2)
            def _():
                copies[0].wait_recv()

            @pl.when(t == 3)
            def _():
                copies[1].wait_recv()

            left_ok = (c > 0) | (s > 0)
            right_ok = (c < nq // GROUP - 1) | (s < GROUP - 1)
            here = meta[s]
            gate = jnp.where(
                hl == 0, here[4:5, :], jnp.where(hl == 1, here[5:6, :], here[6:7, :])
            )
            for part in range(2):
                row = pl.multiple_of(s * slab + part * half, half)
                wait_for(qb.at[:, pl.ds(row, half), :], q_sem.at[s * 2 + part])
                qv = qb[0, pl.ds(row, half), :]
                first = pl.multiple_of(s * slab, slab)
                keys = kv[0, pl.ds(first, 3 * slab), :]
                values = kv[1, pl.ds(first, 3 * slab), :]
                scores = lax.dot_general(
                    qv, keys, (((1,), (1,)), ((), ())), preferred_element_type=jnp.float32
                )
                parts = [scores[:, i * slab : (i + 1) * slab] for i in range(3)]
                tops = [jnp.max(x, axis=1, keepdims=True) for x in parts]
                top = jnp.maximum(
                    tops[1],
                    jnp.maximum(jnp.where(left_ok, tops[0], NEG), jnp.where(right_ok, tops[2], NEG)),
                )
                shifts = (jnp.where(left_ok, top, FAR), top, jnp.where(right_ok, top, FAR))
                probs = jnp.concatenate(
                    [jnp.exp2((x - y) * SCALE).astype(jnp.bfloat16) for x, y in zip(parts, shifts)],
                    axis=1,
                )
                both = jnp.dot(
                    probs, jnp.concatenate([values, ones], axis=1),
                    preferred_element_type=jnp.float32,
                )
                result = both[:, :HD] / both[:, HD:]

                chosen = jnp.concatenate(
                    [
                        jnp.broadcast_to(here[i : i + 1, :], (128, 128)).T
                        for i in range(part * half // 128, (part + 1) * half // 128)
                    ],
                    axis=0,
                )
                cross = jnp.zeros((half, L), jnp.float32)
                for p in range(NPROMPT):
                    one = lax.dot_general(
                        qv, pk[p][...], (((1,), (1,)), ((), ())),
                        preferred_element_type=jnp.float32,
                    )
                    cross = jnp.where(chosen == float(p), one, cross)
                cross_top = jnp.max(cross, axis=1, keepdims=True)
                weights = jnp.exp2((cross - cross_top) * SCALE)
                total = jnp.sum(weights, axis=1, keepdims=True)
                masked = jnp.concatenate(
                    [
                        jnp.where(chosen == float(p), weights, 0.0).astype(jnp.bfloat16)
                        for p in range(NPROMPT)
                    ],
                    axis=1,
                )
                stacked = jnp.concatenate([pkv[p, 1] for p in range(NPROMPT)], axis=0)
                result = result + jnp.dot(
                    masked, stacked, preferred_element_type=jnp.float32
                ) / total
                ob[pl.ds(row, half), :] = (gate * result).astype(jnp.bfloat16)

                target = lax.rem(c * GROUP + s + 1, nq)
                for i in range(nz // 2):
                    z2 = part * (nz // 2) + i
                    src = ob.at[pl.ds(pl.multiple_of(row + i * rows, rows), rows), :]
                    dst = out.at[:, pl.ds(head_col, HD)]
                    mine = (target == q) & (j == z2)

                    @pl.when(mine)
                    def _():
                        pltpu.make_async_copy(src, dst, out_sem).start()

                    @pl.when(jnp.logical_not(mine))
                    def _():
                        pltpu.make_async_remote_copy(
                            src_ref=src, dst_ref=dst, send_sem=out_send, recv_sem=out_sem,
                            device_id={"queue": target, "head": z2}, device_id_type=MESH,
                        ).start()

            return carry

        lax.fori_loop(0, GROUP, one_slab, 0)
        for copy in copies:
            copy.wait_send()
        wait_for(proj.at[:, :, : (heads - 1) * HD], send_sem)

        @pl.when(a == 0)
        def _():
            wait_for(ob, out_send)

        @pl.when(a > 0)
        def _():
            wait_for(ob.at[: GROUP * slab - rows, :], out_send)

    @pl.when(jnp.logical_not(works))
    def _():
        wait_for(proj, send_sem)

    for i in range(GROUP - 1):
        wait_for(meta_src, meta_send.at[i])
    wait_for(out, out_sem)


def solution(mesh):
    nq, nz = mesh.shape["queue"], mesh.shape["head"]

    def per_device(
        projected, prompt_states, region_map, region_prompt, step_index, time_gates, incoming
    ):
        rows, _, channels = projected.shape
        slab = rows * nz
        anywhere = pl.BlockSpec(memory_space=pl.ANY)
        scalars = pl.BlockSpec(memory_space=pltpu.SMEM)
        dma = pltpu.SemaphoreType.DMA

        def kernel(*refs):
            attention_kernel(nq, nz, *refs)

        moved = pl.pallas_call(
            kernel,
            out_shape=jax.ShapeDtypeStruct((rows, channels), jnp.bfloat16),
            in_specs=[anywhere, anywhere, anywhere, scalars, scalars, anywhere],
            out_specs=anywhere,
            scratch_shapes=[
                pltpu.VMEM((2, (GROUP + 2) * slab, HD), jnp.bfloat16),
                pltpu.VMEM((1, GROUP * slab, HD), jnp.bfloat16),
                pltpu.VMEM((GROUP * slab, HD), jnp.bfloat16),
                pltpu.VMEM((NPROMPT, 2, L, HD), jnp.bfloat16),
                pltpu.VMEM(region_map.shape, jnp.int32),
                pltpu.VMEM(time_gates.shape, jnp.float32),
                pltpu.VMEM((8, 128), jnp.float32),
                pltpu.VMEM((GROUP, 8, 128), jnp.float32),
                dma((GROUP,)),
                dma((2 * GROUP,)),
                dma((2,)),
                dma,
                dma,
                dma((3,)),
                dma,
                dma((2,)),
                dma((GROUP - 1,)),
                dma,
            ],
            compiler_params=pltpu.CompilerParams(
                collective_id=0, has_side_effects=True, vmem_limit_bytes=48 * 1024 * 1024
            ),
        )(
            projected.transpose(1, 0, 2), prompt_states, region_map, region_prompt, step_index,
            time_gates,
        )
        return jnp.where(lax.axis_index("queue") == 0, incoming, moved)

    return jax.shard_map(
        per_device,
        mesh=mesh,
        in_specs=(
            P(("queue", "head"), None, None),
            P(None, None, None, "head"),
            P("queue", None),
            P("queue", None),
            P("queue"),
            P(None, "head"),
            P("head", None),
        ),
        out_specs=P(("queue", "head"), None),
        check_vma=False,
    )
```

```python
import math

import jax
import jax.numpy as jnp
from jax import lax
from jax.experimental import pallas as pl
from jax.experimental.pallas import tpu as pltpu
from jax.sharding import PartitionSpec as P

HD = 128
L = 128
R = 4
NPROMPT = 8
GROUP = 4
PER = 3

NEG = -1e30
FAR = 1e30
SCALE = math.log2(math.e) / math.sqrt(HD)
THROTTLE = False
FARKV = True
FARQ = False
MESH = pl.DeviceIdType.MESH


def free_place(z):
    upper = (z == 1) | (z == 2) | (z == 4) | (z == 7)
    return jnp.where(upper, 3, 1)


def wrapped(value, count):
    return jnp.where(value >= count, value - count, jnp.where(value < 0, value + count, value))


def wait_for(ref, sem):
    pltpu.make_async_copy(ref, ref, sem).wait()


def attention_kernel(
    nq, nz,
    proj, prompts, rmap, rprompt, step, gates,
    out,
    kv, qb, ob, pkv, rmap_v, gates_v, meta_src, meta,
    edge_sem, kv_sem, q_sem, halo_sem, meta_sem, out_sem, local_sem,
    kv_send, q_send, halo_send, meta_send, out_send,
):
    rows = proj.shape[1]
    slab = rows * nz
    half = slab // 2
    heads = PER * nz
    ring = 2 * nz
    q = lax.axis_index("queue")
    j = lax.axis_index("head")
    c = lax.div(q, GROUP)
    base = c * GROUP
    a = q - base
    arc = jnp.where(a >= 2, 1, 0)
    core = a - 2 * arc
    z = arc * nz + j
    free = free_place(j)
    works = a != free
    hl = a - jnp.where(a > free, 1, 0)
    right = wrapped(q + GROUP, nq)
    left = wrapped(q - GROUP, nq)

    barrier = pltpu.get_barrier_semaphore()

    def greet(chip, k):
        upper = jnp.where(chip >= nz, 1, 0)
        pl.semaphore_signal(
            barrier, inc=1,
            device_id={"queue": base + 2 * upper + k, "head": chip - nz * upper},
            device_id_type=MESH,
        )

    def greet_chip(m, carry):
        chip = wrapped(z + m, ring)
        greet(chip, 0)
        greet(chip, 1)
        return carry

    lax.fori_loop(1, ring, greet_chip, 0)
    greet(z, 1 - core)
    for side in (left, right):
        pl.semaphore_signal(
            barrier, inc=1, device_id={"queue": side, "head": j}, device_id_type=MESH
        )
    map_copy = pltpu.make_async_copy(rmap, rmap_v, local_sem.at[0])
    gate_copy = pltpu.make_async_copy(gates, gates_v, local_sem.at[1])
    lane = pl.multiple_of(jnp.minimum(hl, PER - 1) * HD, HD)
    prompt_copy = pltpu.make_async_copy(
        prompts.at[:, :, :, pl.ds(lane, HD)], pkv, local_sem.at[2]
    )
    map_copy.start()
    gate_copy.start()
    prompt_copy.start()
    pl.semaphore_wait(barrier, 2 * ring + 1)

    def spread(first, last, dst, send_sem, recv_sem, far):
        def piece(chip, k):
            upper = jnp.where(chip >= nz, 1, 0)
            z2 = chip - nz * upper
            a2 = 2 * upper + k
            free2 = free_place(z2)
            hl2 = a2 - jnp.where(a2 > free2, 1, 0)
            col = pl.multiple_of((z2 * PER + jnp.minimum(hl2, PER - 1)) * HD, HD)
            return a2 != free2, base + a2, z2, proj.at[first:last, :, pl.ds(col, HD)]

        def send(chip, k):
            real, q2, z2, src = piece(chip, k)

            def go():
                pltpu.make_async_remote_copy(
                    src_ref=src, dst_ref=dst, send_sem=send_sem, recv_sem=recv_sem,
                    device_id={"queue": q2, "head": z2}, device_id_type=MESH,
                ).start()

            if k == 0:
                go()
            else:
                pl.when(real)(go)

        def both_ways(m, carry):
            d = nz - m if far else m
            for off in (d, -d):
                chip = wrapped(z + off, ring)
                send(chip, 0)
                send(chip, 1)
            return carry

        @pl.when(works)
        def _():
            pltpu.make_async_copy(piece(z, core)[3], dst, recv_sem).start()

        for k in range(2):
            @pl.when((core != k) & ((k == 0) | (2 * arc + 1 != free)))
            def _():
                real, q2, z2, src = piece(z, k)
                pltpu.make_async_remote_copy(
                    src_ref=src, dst_ref=dst, send_sem=send_sem, recv_sem=recv_sem,
                    device_id={"queue": q2, "head": z2}, device_id_type=MESH,
                ).start()

        opposite = wrapped(z + nz, ring)
        if far:
            send(opposite, 0)
            send(opposite, 1)
        lax.fori_loop(1, nz, both_ways, 0)
        if not far:
            send(opposite, 0)
            send(opposite, 1)

    def sent(first, last, sem):
        @pl.when(works)
        def _():
            wait_for(proj.at[first:last, :, : (heads - 1) * HD], sem)

        @pl.when(jnp.logical_not(works))
        def _():
            wait_for(proj.at[first:last], sem)

    kv_row = pl.multiple_of((a + 1) * slab + j * rows, rows)
    kv_dst = kv.at[:, pl.ds(kv_row, rows), :]
    at_edge = (a == 0) | (a == GROUP - 1)

    @pl.when(at_edge)
    def _():
        spread(1, 3, kv_dst, kv_send, edge_sem.at[jnp.where(a == 0, 0, 1), j], FARKV)

    @pl.when(jnp.logical_not(at_edge))
    def _():
        spread(1, 3, kv_dst, kv_send, kv_sem.at[core], FARKV)

    map_copy.wait()
    gate_copy.wait()
    regions = rmap_v[...]
    token_prompt = jnp.zeros(regions.shape, jnp.int32)
    for r in range(R):
        token_prompt = jnp.where(regions == r, rprompt[0, r], token_prompt)
    token_prompt = token_prompt.astype(jnp.float32)
    for i in range(slab // 128):
        meta_src[i : i + 1, :] = token_prompt[:, i * 128 : (i + 1) * 128]
    table = gates_v[...]
    picked = lax.broadcasted_iota(jnp.int32, table.shape, 0) == step[0]
    gate_row = jnp.sum(jnp.where(picked, table, 0.0), axis=0, keepdims=True)
    for i in range(PER):
        meta_src[4 + i : 5 + i, :] = gate_row[:, i * HD : (i + 1) * HD]
    meta_src[7:8, :] = jnp.zeros((1, 128), jnp.float32)
    pltpu.make_async_copy(meta_src, meta.at[a], meta_sem).start()
    for i in range(1, GROUP):
        pltpu.make_async_remote_copy(
            src_ref=meta_src, dst_ref=meta.at[a], send_sem=meta_send.at[i - 1], recv_sem=meta_sem,
            device_id={"queue": base + wrapped(a + i, GROUP), "head": j},
            device_id_type=MESH,
        ).start()

    if THROTTLE:
        sent(1, 3, kv_send)
    q_row = pl.multiple_of(a * slab + j * rows, rows)
    spread(
        0, 1, qb.at[:, pl.ds(q_row, rows), :], q_send,
        q_sem.at[a * 2 + jnp.where(j >= nz // 2, 1, 0)], FARQ,
    )

    @pl.when(works)
    def _():
        def halo(side, n):
            src, dst, to = ((1, GROUP + 1, left), (GROUP, 0, right))[side]
            return pltpu.make_async_remote_copy(
                src_ref=kv.at[:, pl.ds(pl.multiple_of(src * slab + n * rows, rows), rows), :],
                dst_ref=kv.at[:, pl.ds(pl.multiple_of(dst * slab + n * rows, rows), rows), :],
                send_sem=halo_send.at[side], recv_sem=halo_sem.at[side],
                device_id={"queue": to, "head": j}, device_id_type=MESH,
            )

        def forward(n, carry):
            for side in range(2):
                src = (1, GROUP)[side]
                wait_for(
                    kv.at[:, pl.ds(pl.multiple_of(src * slab + n * rows, rows), rows), :],
                    edge_sem.at[side, n],
                )
                halo(side, n).start()
            return carry

        lax.fori_loop(0, nz, forward, 0)
        for s in range(2):
            wait_for(kv.at[:, (s + 2) * slab : (s + 3) * slab, :], kv_sem.at[s])
        wait_for(meta, meta_sem)
        prompt_copy.wait()
        head_col = pl.multiple_of((j * PER + hl) * HD, HD)
        pk = [pkv.at[p, 0] for p in range(NPROMPT)]
        ones = jnp.ones((3 * slab, HD), jnp.bfloat16)
        within = jnp.where(j >= nz // 2, j - nz // 2, j)
        mine4 = 2 * arc + jnp.where(j >= nz // 2, 1, 0)
        toward = jnp.where(within >= nz // 4, 1, 3)

        def one_block(t, carry):
            turn = jnp.where(t >= 6, 3, jnp.where(t >= 4, 2, jnp.where(t >= 2, 1, 0)))
            quarter = wrapped(
                mine4
                + jnp.where(turn == 0, 2, jnp.where(turn == 1, toward, jnp.where(turn == 2, 4 - toward, 0))),
                4,
            )
            side = jnp.where(quarter >= 2, 1, 0)
            low = quarter - 2 * side
            s = wrapped(2 * side + t - 2 * turn - 1, GROUP)

            @pl.when(t == 0)
            def _():
                wait_for(kv.at[:, (GROUP + 1) * slab :, :], halo_sem.at[0])
                wait_for(kv.at[:, :slab, :], halo_sem.at[1])

            left_ok = (c > 0) | (s > 0)
            right_ok = (c < nq // GROUP - 1) | (s < GROUP - 1)
            here = meta[s]
            gate = jnp.where(
                hl == 0, here[4:5, :], jnp.where(hl == 1, here[5:6, :], here[6:7, :])
            )
            row = pl.multiple_of(s * slab + low * half, half)
            wait_for(qb.at[:, pl.ds(row, half), :], q_sem.at[s * 2 + low])
            qv = qb[0, pl.ds(row, half), :]
            first = pl.multiple_of(s * slab, slab)
            keys = kv[0, pl.ds(first, 3 * slab), :]
            values = kv[1, pl.ds(first, 3 * slab), :]
            scores = lax.dot_general(
                qv, keys, (((1,), (1,)), ((), ())), preferred_element_type=jnp.float32
            )
            parts = [scores[:, i * slab : (i + 1) * slab] for i in range(3)]
            tops = [jnp.max(x, axis=1, keepdims=True) for x in parts]
            top = jnp.maximum(
                tops[1],
                jnp.maximum(jnp.where(left_ok, tops[0], NEG), jnp.where(right_ok, tops[2], NEG)),
            )
            shifts = (jnp.where(left_ok, top, FAR), top, jnp.where(right_ok, top, FAR))
            probs = jnp.concatenate(
                [jnp.exp2((x - y) * SCALE).astype(jnp.bfloat16) for x, y in zip(parts, shifts)],
                axis=1,
            )
            both = jnp.dot(
                probs, jnp.concatenate([values, ones], axis=1),
                preferred_element_type=jnp.float32,
            )
            result = both[:, :HD] / both[:, HD:]

            chosen = jnp.concatenate(
                [
                    jnp.broadcast_to(
                        jnp.where(low == 0, here[i : i + 1, :], here[i + 2 : i + 3, :]), (128, 128)
                    ).T
                    for i in range(2)
                ],
                axis=0,
            )
            cross = jnp.zeros((half, L), jnp.float32)
            for p in range(NPROMPT):
                one = lax.dot_general(
                    qv, pk[p][...], (((1,), (1,)), ((), ())),
                    preferred_element_type=jnp.float32,
                )
                cross = jnp.where(chosen == float(p), one, cross)
            cross_top = jnp.max(cross, axis=1, keepdims=True)
            weights = jnp.exp2((cross - cross_top) * SCALE)
            total = jnp.sum(weights, axis=1, keepdims=True)
            masked = jnp.concatenate(
                [
                    jnp.where(chosen == float(p), weights, 0.0).astype(jnp.bfloat16)
                    for p in range(NPROMPT)
                ],
                axis=1,
            )
            stacked = jnp.concatenate([pkv[p, 1] for p in range(NPROMPT)], axis=0)
            result = result + jnp.dot(
                masked, stacked, preferred_element_type=jnp.float32
            ) / total
            ob[pl.ds(row, half), :] = (gate * result).astype(jnp.bfloat16)

            target = wrapped(base + s + 1, nq)
            for i in range(nz // 2):
                z2 = low * (nz // 2) + i
                src = ob.at[pl.ds(pl.multiple_of(row + i * rows, rows), rows), :]
                dst = out.at[:, pl.ds(head_col, HD)]
                mine = (target == q) & (j == z2)

                @pl.when(mine)
                def _():
                    pltpu.make_async_copy(src, dst, out_sem).start()

                @pl.when(jnp.logical_not(mine))
                def _():
                    pltpu.make_async_remote_copy(
                        src_ref=src, dst_ref=dst, send_sem=out_send, recv_sem=out_sem,
                        device_id={"queue": target, "head": z2}, device_id_type=MESH,
                    ).start()

            return carry

        lax.fori_loop(0, 2 * GROUP, one_block, 0)
        for side in range(2):
            wait_for(kv.at[:, :slab, :], halo_send.at[side])

        @pl.when(a == 0)
        def _():
            wait_for(ob, out_send)

        @pl.when(a > 0)
        def _():
            wait_for(ob.at[: GROUP * slab - rows, :], out_send)

    @pl.when(jnp.logical_not(works))
    def _():
        wait_for(meta, meta_sem)
        prompt_copy.wait()

    if not THROTTLE:
        sent(1, 3, kv_send)
    sent(0, 1, q_send)
    for i in range(GROUP - 1):
        wait_for(meta_src, meta_send.at[i])
    wait_for(out, out_sem)


def solution(mesh):
    nq, nz = mesh.shape["queue"], mesh.shape["head"]

    def per_device(
        projected, prompt_states, region_map, region_prompt, step_index, time_gates, incoming
    ):
        rows, _, channels = projected.shape
        slab = rows * nz
        anywhere = pl.BlockSpec(memory_space=pl.ANY)
        scalars = pl.BlockSpec(memory_space=pltpu.SMEM)
        dma = pltpu.SemaphoreType.DMA

        def kernel(*refs):
            attention_kernel(nq, nz, *refs)

        moved = pl.pallas_call(
            kernel,
            out_shape=jax.ShapeDtypeStruct((rows, channels), jnp.bfloat16),
            in_specs=[anywhere, anywhere, anywhere, scalars, scalars, anywhere],
            out_specs=anywhere,
            scratch_shapes=[
                pltpu.VMEM((2, (GROUP + 2) * slab, HD), jnp.bfloat16),
                pltpu.VMEM((1, GROUP * slab, HD), jnp.bfloat16),
                pltpu.VMEM((GROUP * slab, HD), jnp.bfloat16),
                pltpu.VMEM((NPROMPT, 2, L, HD), jnp.bfloat16),
                pltpu.VMEM(region_map.shape, jnp.int32),
                pltpu.VMEM(time_gates.shape, jnp.float32),
                pltpu.VMEM((8, 128), jnp.float32),
                pltpu.VMEM((GROUP, 8, 128), jnp.float32),
                dma((2, nz)),
                dma((2,)),
                dma((2 * GROUP,)),
                dma((2,)),
                dma,
                dma,
                dma((3,)),
                dma,
                dma,
                dma((2,)),
                dma((GROUP - 1,)),
                dma,
            ],
            compiler_params=pltpu.CompilerParams(
                collective_id=0, has_side_effects=True, vmem_limit_bytes=63_400_000
            ),
        )(
            projected.transpose(1, 0, 2), prompt_states, region_map, region_prompt, step_index,
            time_gates,
        )
        return jnp.where(lax.axis_index("queue") == 0, incoming, moved)

    return jax.shard_map(
        per_device,
        mesh=mesh,
        in_specs=(
            P(("queue", "head"), None, None),
            P(None, None, None, "head"),
            P("queue", None),
            P("queue", None),
            P("queue"),
            P(None, "head"),
            P("head", None),
        ),
        out_specs=P(("queue", "head"), None),
        check_vma=False,
    )
```

```python
import math

import jax
import jax.numpy as jnp
from jax import lax
from jax.experimental import pallas as pl
from jax.experimental.pallas import tpu as pltpu
from jax.sharding import PartitionSpec as P

HD = 128
L = 128
R = 4
NPROMPT = 8
GROUP = 4
PER = 3

NEG = -1e30
FAR = 1e30
SCALE = math.log2(math.e) / math.sqrt(HD)
THROTTLE = False
MESH = pl.DeviceIdType.MESH


def free_place(z):
    upper = (z == 1) | (z == 3) | (z == 4) | (z == 7)
    return jnp.where(upper, 3, 1)


def wrapped(value, count):
    return jnp.where(value >= count, value - count, jnp.where(value < 0, value + count, value))


def wait_for(ref, sem):
    pltpu.make_async_copy(ref, ref, sem).wait()


def attention_kernel(
    nq, nz,
    proj, prompts, rmap, rprompt, step, gates,
    out,
    kv, qb, ob, pkv, rmap_v, gates_v, meta_src, meta,
    kv_sem, ready, q_sem, halo_sem, meta_sem, out_sem, local_sem,
    kv_send, q_send, halo_send, meta_send, out_send,
):
    rows = proj.shape[1]
    slab = rows * nz
    half = slab // 2
    heads = PER * nz
    ring = 2 * nz
    q = lax.axis_index("queue")
    j = lax.axis_index("head")
    c = lax.div(q, GROUP)
    base = c * GROUP
    a = q - base
    arc = jnp.where(a >= 2, 1, 0)
    core = a - 2 * arc
    z = arc * nz + j
    free = free_place(j)
    works = a != free
    hl = a - jnp.where(a > free, 1, 0)
    has_left = c > 0
    has_right = q + GROUP < nq
    sides = ((has_left, q - GROUP), (has_right, q + GROUP))

    barrier = pltpu.get_barrier_semaphore()

    def greet(chip, k):
        upper = jnp.where(chip >= nz, 1, 0)
        pl.semaphore_signal(
            barrier, inc=1,
            device_id={"queue": base + 2 * upper + k, "head": chip - nz * upper},
            device_id_type=MESH,
        )

    for off in (1, -1):
        chip = wrapped(z + off, ring)
        greet(chip, 0)
        greet(chip, 1)
    greet(z, 1 - core)
    for there, other in sides:

        @pl.when(there)
        def _():
            pl.semaphore_signal(
                barrier, inc=1, device_id={"queue": other, "head": j}, device_id_type=MESH
            )

    map_copy = pltpu.make_async_copy(rmap, rmap_v, local_sem.at[0])
    gate_copy = pltpu.make_async_copy(gates, gates_v, local_sem.at[1])
    lane = pl.multiple_of(jnp.minimum(hl, PER - 1) * HD, HD)
    prompt_copy = pltpu.make_async_copy(
        prompts.at[:, :, :, pl.ds(lane, HD)], pkv, local_sem.at[2]
    )
    map_copy.start()
    gate_copy.start()
    prompt_copy.start()
    both_sides = has_left & has_right

    @pl.when(both_sides)
    def _():
        pl.semaphore_wait(barrier, 7)

    @pl.when(jnp.logical_not(both_sides))
    def _():
        pl.semaphore_wait(barrier, 6)

    for there, slot in ((has_left, 0), (has_right, GROUP + 1)):

        @pl.when(jnp.logical_not(there))
        def _():
            kv[:, slot * slab : (slot + 1) * slab, :] = jnp.zeros((2, slab, HD), jnp.bfloat16)


    def tell(n):
        for off in (2**n, -(2**n)):
            chip = wrapped(z + off, ring)
            upper = jnp.where(chip >= nz, 1, 0)
            pl.semaphore_signal(
                ready.at[n], inc=1,
                device_id={"queue": base + 2 * upper + core, "head": chip - nz * upper},
                device_id_type=MESH,
            )

    rounds = nz.bit_length() - 1
    tell(0)

    def spread(first, last, dst, send_sem, recv_sem, opening):
        def piece(chip, k):
            upper = jnp.where(chip >= nz, 1, 0)
            z2 = chip - nz * upper
            a2 = 2 * upper + k
            free2 = free_place(z2)
            hl2 = a2 - jnp.where(a2 > free2, 1, 0)
            col = pl.multiple_of((z2 * PER + jnp.minimum(hl2, PER - 1)) * HD, HD)
            return a2 != free2, base + a2, z2, proj.at[first:last, :, pl.ds(col, HD)]

        def send(chip, k):
            real, q2, z2, src = piece(chip, k)

            def go():
                pltpu.make_async_remote_copy(
                    src_ref=src, dst_ref=dst, send_sem=send_sem, recv_sem=recv_sem,
                    device_id={"queue": q2, "head": z2}, device_id_type=MESH,
                ).start()

            if k == 0:
                go()
            else:
                pl.when(real)(go)

        def both_ways(m, carry):
            for off in (m, -m):
                chip = wrapped(z + off, ring)
                send(chip, 0)
                send(chip, 1)
            return carry

        @pl.when(works)
        def _():
            pltpu.make_async_copy(piece(z, core)[3], dst, recv_sem).start()

        for k in range(2):
            @pl.when((core != k) & ((k == 0) | (2 * arc + 1 != free)))
            def _():
                real, q2, z2, src = piece(z, k)
                pltpu.make_async_remote_copy(
                    src_ref=src, dst_ref=dst, send_sem=send_sem, recv_sem=recv_sem,
                    device_id={"queue": q2, "head": z2}, device_id_type=MESH,
                ).start()

        if opening:
            for n in range(rounds):
                lax.fori_loop(2**n // 2 + 1, 2**n + 1, both_ways, 0)
                pl.semaphore_wait(ready.at[n], 2)
                if n + 1 < rounds:
                    tell(n + 1)
            lax.fori_loop(nz // 2 + 1, nz, both_ways, 0)
        else:
            lax.fori_loop(1, nz, both_ways, 0)
        opposite = wrapped(z + nz, ring)
        send(opposite, 0)
        send(opposite, 1)

    def sent(first, last, sem):
        @pl.when(works)
        def _():
            wait_for(proj.at[first:last, :, : (heads - 1) * HD], sem)

        @pl.when(jnp.logical_not(works))
        def _():
            wait_for(proj.at[first:last], sem)

    kv_row = pl.multiple_of((a + 1) * slab + j * rows, rows)
    kv_dst = kv.at[:, pl.ds(kv_row, rows), :]
    spread(1, 3, kv_dst, kv_send, kv_sem.at[a, j], True)

    map_copy.wait()
    gate_copy.wait()
    regions = rmap_v[...]
    token_prompt = jnp.zeros(regions.shape, jnp.int32)
    for r in range(R):
        token_prompt = jnp.where(regions == r, rprompt[0, r], token_prompt)
    token_prompt = token_prompt.astype(jnp.float32)
    for i in range(slab // 128):
        meta_src[i : i + 1, :] = token_prompt[:, i * 128 : (i + 1) * 128]
    table = gates_v[...]
    picked = lax.broadcasted_iota(jnp.int32, table.shape, 0) == step[0]
    gate_row = jnp.sum(jnp.where(picked, table, 0.0), axis=0, keepdims=True)
    for i in range(PER):
        meta_src[4 + i : 5 + i, :] = gate_row[:, i * HD : (i + 1) * HD]
    meta_src[7:8, :] = jnp.zeros((1, 128), jnp.float32)
    pltpu.make_async_copy(meta_src, meta.at[a], meta_sem).start()
    for i in range(1, GROUP):
        pltpu.make_async_remote_copy(
            src_ref=meta_src, dst_ref=meta.at[a], send_sem=meta_send.at[i - 1], recv_sem=meta_sem,
            device_id={"queue": base + wrapped(a + i, GROUP), "head": j},
            device_id_type=MESH,
        ).start()

    if THROTTLE:
        sent(1, 3, kv_send)
    q_row = pl.multiple_of(a * slab + j * rows, rows)
    spread(
        0, 1, qb.at[:, pl.ds(q_row, rows), :], q_send,
        q_sem.at[a * 2 + jnp.where(j >= nz // 2, 1, 0)], False,
    )

    @pl.when(works)
    def _():
        def halo(side, n):
            src, dst, to = ((1, GROUP + 1, q - GROUP), (GROUP, 0, q + GROUP))[side]
            return pltpu.make_async_remote_copy(
                src_ref=kv.at[:, pl.ds(pl.multiple_of(src * slab + n * rows, rows), rows), :],
                dst_ref=kv.at[:, pl.ds(pl.multiple_of(dst * slab + n * rows, rows), rows), :],
                send_sem=halo_send.at[side], recv_sem=halo_sem.at[side],
                device_id={"queue": to, "head": j}, device_id_type=MESH,
            )

        def forward(n, carry):
            for side in range(2):
                src = (1, GROUP)[side]
                wait_for(
                    kv.at[:, pl.ds(pl.multiple_of(src * slab + n * rows, rows), rows), :],
                    kv_sem.at[src - 1, n],
                )


                @pl.when(sides[side][0])
                def _():
                    halo(side, n).start()

            for s in range(1, GROUP - 1):
                wait_for(
                    kv.at[:, pl.ds(pl.multiple_of((s + 1) * slab + n * rows, rows), rows), :],
                    kv_sem.at[s, n],
                )
            return carry

        lax.fori_loop(0, nz, forward, 0)
        wait_for(meta, meta_sem)
        prompt_copy.wait()
        head_col = pl.multiple_of((j * PER + hl) * HD, HD)
        pk = [pkv.at[p, 0] for p in range(NPROMPT)]
        ones = jnp.ones((3 * slab, HD), jnp.bfloat16)
        within = jnp.where(j >= nz // 2, j - nz // 2, j)
        mine4 = 2 * arc + jnp.where(j >= nz // 2, 1, 0)
        toward = jnp.where(within >= nz // 4, 1, 3)

        def one_block(t, carry):
            turn = jnp.where(t >= 6, 3, jnp.where(t >= 4, 2, jnp.where(t >= 2, 1, 0)))
            quarter = wrapped(
                mine4
                + jnp.where(turn == 0, 2, jnp.where(turn == 1, toward, jnp.where(turn == 2, 4 - toward, 0))),
                4,
            )
            side = jnp.where(quarter >= 2, 1, 0)
            low = quarter - 2 * side
            s = wrapped(2 * side + t - 2 * turn - 1, GROUP)

            @pl.when(t == 0)
            def _():
                @pl.when(has_right)
                def _():
                    wait_for(kv.at[:, (GROUP + 1) * slab :, :], halo_sem.at[0])

                @pl.when(has_left)
                def _():
                    wait_for(kv.at[:, :slab, :], halo_sem.at[1])


            left_ok = has_left | (s > 0)
            right_ok = has_right | (s < GROUP - 1)
            here = meta[s]
            gate = jnp.where(
                hl == 0, here[4:5, :], jnp.where(hl == 1, here[5:6, :], here[6:7, :])
            )
            row = pl.multiple_of(s * slab + low * half, half)
            wait_for(qb.at[:, pl.ds(row, half), :], q_sem.at[s * 2 + low])
            qv = qb[0, pl.ds(row, half), :]
            first = pl.multiple_of(s * slab, slab)
            keys = kv[0, pl.ds(first, 3 * slab), :]
            values = kv[1, pl.ds(first, 3 * slab), :]
            scores = lax.dot_general(
                qv, keys, (((1,), (1,)), ((), ())), preferred_element_type=jnp.float32
            )
            parts = [scores[:, i * slab : (i + 1) * slab] for i in range(3)]
            tops = [jnp.max(x, axis=1, keepdims=True) for x in parts]
            top = jnp.maximum(
                tops[1],
                jnp.maximum(jnp.where(left_ok, tops[0], NEG), jnp.where(right_ok, tops[2], NEG)),
            )
            shifts = (jnp.where(left_ok, top, FAR), top, jnp.where(right_ok, top, FAR))
            probs = jnp.concatenate(
                [jnp.exp2((x - y) * SCALE).astype(jnp.bfloat16) for x, y in zip(parts, shifts)],
                axis=1,
            )
            both = jnp.dot(
                probs, jnp.concatenate([values, ones], axis=1),
                preferred_element_type=jnp.float32,
            )
            result = both[:, :HD] / both[:, HD:]

            chosen = jnp.concatenate(
                [
                    jnp.broadcast_to(
                        jnp.where(low == 0, here[i : i + 1, :], here[i + 2 : i + 3, :]), (128, 128)
                    ).T
                    for i in range(2)
                ],
                axis=0,
            )
            cross = jnp.zeros((half, L), jnp.float32)
            for p in range(NPROMPT):
                one = lax.dot_general(
                    qv, pk[p][...], (((1,), (1,)), ((), ())),
                    preferred_element_type=jnp.float32,
                )
                cross = jnp.where(chosen == float(p), one, cross)
            cross_top = jnp.max(cross, axis=1, keepdims=True)
            weights = jnp.exp2((cross - cross_top) * SCALE)
            total = jnp.sum(weights, axis=1, keepdims=True)
            masked = jnp.concatenate(
                [
                    jnp.where(chosen == float(p), weights, 0.0).astype(jnp.bfloat16)
                    for p in range(NPROMPT)
                ],
                axis=1,
            )
            stacked = jnp.concatenate([pkv[p, 1] for p in range(NPROMPT)], axis=0)
            result = result + jnp.dot(
                masked, stacked, preferred_element_type=jnp.float32
            ) / total
            ob[pl.ds(row, half), :] = (gate * result).astype(jnp.bfloat16)

            target = base + s + 1
            for i in range(nz // 2):
                z2 = low * (nz // 2) + i
                src = ob.at[pl.ds(pl.multiple_of(row + i * rows, rows), rows), :]
                dst = out.at[:, pl.ds(head_col, HD)]
                mine = (target == q) & (j == z2)

                @pl.when(mine)
                def _():
                    pltpu.make_async_copy(src, dst, out_sem).start()

                @pl.when(jnp.logical_not(mine) & (target < nq))
                def _():
                    pltpu.make_async_remote_copy(
                        src_ref=src, dst_ref=dst, send_sem=out_send, recv_sem=out_sem,
                        device_id={"queue": target, "head": z2}, device_id_type=MESH,
                    ).start()

            return carry

        lax.fori_loop(0, 2 * GROUP, one_block, 0)
        for side in range(2):

            @pl.when(sides[side][0])
            def _():
                wait_for(kv.at[:, :slab, :], halo_send.at[side])

        for slabs, there in ((GROUP, has_right), (GROUP - 1, jnp.logical_not(has_right))):

            @pl.when(there & (a == 0))
            def _():
                wait_for(ob.at[: slabs * slab, :], out_send)

            @pl.when(there & (a > 0))
            def _():
                wait_for(ob.at[: slabs * slab - rows, :], out_send)

    @pl.when(jnp.logical_not(works))
    def _():
        wait_for(meta, meta_sem)
        prompt_copy.wait()

    if not THROTTLE:
        sent(1, 3, kv_send)
    sent(0, 1, q_send)
    for i in range(GROUP - 1):
        wait_for(meta_src, meta_send.at[i])

    @pl.when(q > 0)
    def _():
        wait_for(out, out_sem)


def solution(mesh):
    nq, nz = mesh.shape["queue"], mesh.shape["head"]

    def per_device(
        projected, prompt_states, region_map, region_prompt, step_index, time_gates, incoming
    ):
        rows, _, channels = projected.shape
        slab = rows * nz
        anywhere = pl.BlockSpec(memory_space=pl.ANY)
        scalars = pl.BlockSpec(memory_space=pltpu.SMEM)
        dma = pltpu.SemaphoreType.DMA

        def kernel(*refs):
            attention_kernel(nq, nz, *refs)

        moved = pl.pallas_call(
            kernel,
            out_shape=jax.ShapeDtypeStruct((rows, channels), jnp.bfloat16),
            in_specs=[anywhere, anywhere, anywhere, scalars, scalars, anywhere],
            out_specs=anywhere,
            scratch_shapes=[
                pltpu.VMEM((2, (GROUP + 2) * slab, HD), jnp.bfloat16),
                pltpu.VMEM((1, GROUP * slab, HD), jnp.bfloat16),
                pltpu.VMEM((GROUP * slab, HD), jnp.bfloat16),
                pltpu.VMEM((NPROMPT, 2, L, HD), jnp.bfloat16),
                pltpu.VMEM(region_map.shape, jnp.int32),
                pltpu.VMEM(time_gates.shape, jnp.float32),
                pltpu.VMEM((8, 128), jnp.float32),
                pltpu.VMEM((GROUP, 8, 128), jnp.float32),
                dma((GROUP, nz)),
                pltpu.SemaphoreType.REGULAR((3,)),
                dma((2 * GROUP,)),
                dma((2,)),
                dma,
                dma,
                dma((3,)),
                dma,
                dma,
                dma((2,)),
                dma((GROUP - 1,)),
                dma,
            ],
            compiler_params=pltpu.CompilerParams(
                collective_id=0, has_side_effects=True, vmem_limit_bytes=63_400_000
            ),
        )(
            projected.transpose(1, 0, 2), prompt_states, region_map, region_prompt, step_index,
            time_gates,
        )
        return jnp.where(lax.axis_index("queue") == 0, incoming, moved)

    return jax.shard_map(
        per_device,
        mesh=mesh,
        in_specs=(
            P(("queue", "head"), None, None),
            P(None, None, None, "head"),
            P("queue", None),
            P("queue", None),
            P("queue"),
            P(None, "head"),
            P("head", None),
        ),
        out_specs=P(("queue", "head"), None),
        check_vma=False,
    )
```

```python
import math

import jax
import jax.numpy as jnp
from jax import lax
from jax.experimental import pallas as pl
from jax.experimental.pallas import tpu as pltpu
from jax.sharding import PartitionSpec as P

HD = 128
L = 128
R = 4
NPROMPT = 8
GROUP = 4
PER = 3

NEG = -1e30
FAR = 1e30
SCALE = math.log2(math.e) / math.sqrt(HD)
THROTTLE = False
MESH = pl.DeviceIdType.MESH


def free_place(z):
    upper = (z == 1) | (z == 3) | (z == 4) | (z == 7)
    return jnp.where(upper, 3, 1)


def wrapped(value, count):
    return jnp.where(value >= count, value - count, jnp.where(value < 0, value + count, value))


def wait_for(ref, sem):
    pltpu.make_async_copy(ref, ref, sem).wait()


def attention_kernel(
    nq, nz,
    proj, prompts, rmap, rprompt, step, gates,
    out,
    kv, qb, ob, pkv, rmap_v, gates_v, meta_src, meta,
    kv_sem, ready, q_sem, halo_sem, meta_sem, out_sem, local_sem,
    kv_send, q_send, halo_send, meta_send, out_send,
):
    rows = proj.shape[1]
    slab = rows * nz
    half = slab // 2
    heads = PER * nz
    ring = 2 * nz
    q = lax.axis_index("queue")
    j = lax.axis_index("head")
    c = lax.div(q, GROUP)
    base = c * GROUP
    a = q - base
    arc = jnp.where(a >= 2, 1, 0)
    core = a - 2 * arc
    z = arc * nz + j
    free = free_place(j)
    works = a != free
    hl = a - jnp.where(a > free, 1, 0)
    has_left = c > 0
    has_right = q + GROUP < nq
    sides = ((has_left, q - GROUP), (has_right, q + GROUP))

    barrier = pltpu.get_barrier_semaphore()

    def greet(chip, k):
        upper = jnp.where(chip >= nz, 1, 0)
        pl.semaphore_signal(
            barrier, inc=1,
            device_id={"queue": base + 2 * upper + k, "head": chip - nz * upper},
            device_id_type=MESH,
        )

    for off in (1, -1):
        chip = wrapped(z + off, ring)
        greet(chip, 0)
        greet(chip, 1)
    greet(z, 1 - core)
    for there, other in sides:

        @pl.when(there)
        def _():
            pl.semaphore_signal(
                barrier, inc=1, device_id={"queue": other, "head": j}, device_id_type=MESH
            )

    map_copy = pltpu.make_async_copy(rmap, rmap_v, local_sem.at[0])
    gate_copy = pltpu.make_async_copy(gates, gates_v, local_sem.at[1])
    lane = pl.multiple_of(jnp.minimum(hl, PER - 1) * HD, HD)
    prompt_copy = pltpu.make_async_copy(
        prompts.at[:, :, :, pl.ds(lane, HD)], pkv, local_sem.at[2]
    )
    map_copy.start()
    gate_copy.start()
    prompt_copy.start()
    both_sides = has_left & has_right

    @pl.when(both_sides)
    def _():
        pl.semaphore_wait(barrier, 7)

    @pl.when(jnp.logical_not(both_sides))
    def _():
        pl.semaphore_wait(barrier, 6)

    for there, slot in ((has_left, 0), (has_right, GROUP + 1)):

        @pl.when(jnp.logical_not(there))
        def _():
            kv[:, slot * slab : (slot + 1) * slab, :] = jnp.zeros((2, slab, HD), jnp.bfloat16)


    def tell(n):
        for off in (2**n, -(2**n)):
            chip = wrapped(z + off, ring)
            upper = jnp.where(chip >= nz, 1, 0)
            pl.semaphore_signal(
                ready.at[n], inc=1,
                device_id={"queue": base + 2 * upper + core, "head": chip - nz * upper},
                device_id_type=MESH,
            )

    rounds = nz.bit_length() - 1
    tell(0)

    def spread(first, last, dst, send_sem, recv_sem, opening):
        def piece(chip, k):
            upper = jnp.where(chip >= nz, 1, 0)
            z2 = chip - nz * upper
            a2 = 2 * upper + k
            free2 = free_place(z2)
            hl2 = a2 - jnp.where(a2 > free2, 1, 0)
            col = pl.multiple_of((z2 * PER + jnp.minimum(hl2, PER - 1)) * HD, HD)
            return a2 != free2, base + a2, z2, proj.at[first:last, :, pl.ds(col, HD)]

        def send(chip, k):
            real, q2, z2, src = piece(chip, k)

            def go():
                pltpu.make_async_remote_copy(
                    src_ref=src, dst_ref=dst, send_sem=send_sem, recv_sem=recv_sem,
                    device_id={"queue": q2, "head": z2}, device_id_type=MESH,
                ).start()

            if k == 0:
                go()
            else:
                pl.when(real)(go)

        def both_ways(m, carry):
            for off in (m, -m):
                chip = wrapped(z + off, ring)
                send(chip, 0)
                send(chip, 1)
            return carry

        @pl.when(works)
        def _():
            pltpu.make_async_copy(piece(z, core)[3], dst, recv_sem).start()

        for k in range(2):
            @pl.when((core != k) & ((k == 0) | (2 * arc + 1 != free)))
            def _():
                real, q2, z2, src = piece(z, k)
                pltpu.make_async_remote_copy(
                    src_ref=src, dst_ref=dst, send_sem=send_sem, recv_sem=recv_sem,
                    device_id={"queue": q2, "head": z2}, device_id_type=MESH,
                ).start()

        if opening:
            for n in range(rounds):
                lax.fori_loop(2**n // 2 + 1, 2**n + 1, both_ways, 0)
                pl.semaphore_wait(ready.at[n], 2)
                if n + 1 < rounds:
                    tell(n + 1)
            lax.fori_loop(nz // 2 + 1, nz, both_ways, 0)
        else:
            lax.fori_loop(1, nz, both_ways, 0)
        opposite = wrapped(z + nz, ring)
        send(opposite, 0)
        send(opposite, 1)

    def sent(first, last, sem):
        @pl.when(works)
        def _():
            wait_for(proj.at[first:last, :, : (heads - 1) * HD], sem)

        @pl.when(jnp.logical_not(works))
        def _():
            wait_for(proj.at[first:last], sem)

    kv_row = pl.multiple_of((a + 1) * slab + j * rows, rows)
    kv_dst = kv.at[:, pl.ds(kv_row, rows), :]
    spread(1, 3, kv_dst, kv_send, kv_sem.at[a, j], True)

    map_copy.wait()
    gate_copy.wait()
    regions = rmap_v[...]
    token_prompt = jnp.zeros(regions.shape, jnp.int32)
    for r in range(R):
        token_prompt = jnp.where(regions == r, rprompt[0, r], token_prompt)
    token_prompt = token_prompt.astype(jnp.float32)
    for i in range(slab // 128):
        meta_src[i : i + 1, :] = token_prompt[:, i * 128 : (i + 1) * 128]
    table = gates_v[...]
    picked = lax.broadcasted_iota(jnp.int32, table.shape, 0) == step[0]
    gate_row = jnp.sum(jnp.where(picked, table, 0.0), axis=0, keepdims=True)
    for i in range(PER):
        meta_src[4 + i : 5 + i, :] = gate_row[:, i * HD : (i + 1) * HD]
    meta_src[7:8, :] = jnp.zeros((1, 128), jnp.float32)
    pltpu.make_async_copy(meta_src, meta.at[a], meta_sem).start()
    for i in range(1, GROUP):
        pltpu.make_async_remote_copy(
            src_ref=meta_src, dst_ref=meta.at[a], send_sem=meta_send.at[i - 1], recv_sem=meta_sem,
            device_id={"queue": base + wrapped(a + i, GROUP), "head": j},
            device_id_type=MESH,
        ).start()

    if THROTTLE:
        sent(1, 3, kv_send)
    q_row = pl.multiple_of(a * slab + j * rows, rows)
    spread(
        0, 1, qb.at[:, pl.ds(q_row, rows), :], q_send,
        q_sem.at[a * 2 + jnp.where(j >= nz // 2, 1, 0)], False,
    )

    @pl.when(works)
    def _():
        def halo(side, n):
            src, dst, to = ((1, GROUP + 1, q - GROUP), (GROUP, 0, q + GROUP))[side]
            return pltpu.make_async_remote_copy(
                src_ref=kv.at[:, pl.ds(pl.multiple_of(src * slab + n * rows, rows), rows), :],
                dst_ref=kv.at[:, pl.ds(pl.multiple_of(dst * slab + n * rows, rows), rows), :],
                send_sem=halo_send.at[side], recv_sem=halo_sem.at[side],
                device_id={"queue": to, "head": j}, device_id_type=MESH,
            )

        def forward(n, carry):
            for side in range(2):
                src = (1, GROUP)[side]
                wait_for(
                    kv.at[:, pl.ds(pl.multiple_of(src * slab + n * rows, rows), rows), :],
                    kv_sem.at[src - 1, n],
                )


                @pl.when(sides[side][0])
                def _():
                    halo(side, n).start()

            for s in range(1, GROUP - 1):
                wait_for(
                    kv.at[:, pl.ds(pl.multiple_of((s + 1) * slab + n * rows, rows), rows), :],
                    kv_sem.at[s, n],
                )
            return carry

        lax.fori_loop(0, nz, forward, 0)
        wait_for(meta, meta_sem)
        prompt_copy.wait()
        head_col = pl.multiple_of((j * PER + hl) * HD, HD)
        pk = [pkv.at[p, 0] for p in range(NPROMPT)]
        ones = jnp.ones((3 * slab, HD), jnp.bfloat16)
        within = jnp.where(j >= nz // 2, j - nz // 2, j)
        mine4 = 2 * arc + jnp.where(j >= nz // 2, 1, 0)

        def one_block(t, carry):
            turn = jnp.where(t >= 6, 3, jnp.where(t >= 4, 2, jnp.where(t >= 2, 1, 0)))
            targets = (
                jnp.where(mine4 == 0, 0, jnp.where(mine4 == 1, 3, jnp.where(mine4 == 2, 0, 0))),
                jnp.where(mine4 == 0, 2, jnp.where(mine4 == 1, 0, jnp.where(mine4 == 2, 3, 2))),
                jnp.where(mine4 == 0, 3, jnp.where(mine4 == 1, 2, jnp.where(mine4 == 2, 1, 1))),
                jnp.where(mine4 == 0, 1, jnp.where(mine4 == 1, 1, jnp.where(mine4 == 2, 2, 3))),
            )
            quarter = jnp.where(turn == 0, targets[0], jnp.where(turn == 1, targets[1], jnp.where(turn == 2, targets[2], targets[3])))
            side = jnp.where(quarter >= 2, 1, 0)
            low = quarter - 2 * side
            s = wrapped(2 * side + t - 2 * turn - 1, GROUP)

            @pl.when(t == 0)
            def _():
                @pl.when(has_right)
                def _():
                    wait_for(kv.at[:, (GROUP + 1) * slab :, :], halo_sem.at[0])

                @pl.when(has_left)
                def _():
                    wait_for(kv.at[:, :slab, :], halo_sem.at[1])


            left_ok = has_left | (s > 0)
            right_ok = has_right | (s < GROUP - 1)
            here = meta[s]
            gate = jnp.where(
                hl == 0, here[4:5, :], jnp.where(hl == 1, here[5:6, :], here[6:7, :])
            )
            row = pl.multiple_of(s * slab + low * half, half)
            wait_for(qb.at[:, pl.ds(row, half), :], q_sem.at[s * 2 + low])
            qv = qb[0, pl.ds(row, half), :]
            first = pl.multiple_of(s * slab, slab)
            keys = kv[0, pl.ds(first, 3 * slab), :]
            values = kv[1, pl.ds(first, 3 * slab), :]
            scores = lax.dot_general(
                qv, keys, (((1,), (1,)), ((), ())), preferred_element_type=jnp.float32
            )
            parts = [scores[:, i * slab : (i + 1) * slab] for i in range(3)]
            tops = [jnp.max(x, axis=1, keepdims=True) for x in parts]
            top = jnp.maximum(
                tops[1],
                jnp.maximum(jnp.where(left_ok, tops[0], NEG), jnp.where(right_ok, tops[2], NEG)),
            )
            shifts = (jnp.where(left_ok, top, FAR), top, jnp.where(right_ok, top, FAR))
            probs = jnp.concatenate(
                [jnp.exp2((x - y) * SCALE).astype(jnp.bfloat16) for x, y in zip(parts, shifts)],
                axis=1,
            )
            both = jnp.dot(
                probs, jnp.concatenate([values, ones], axis=1),
                preferred_element_type=jnp.float32,
            )
            result = both[:, :HD] / both[:, HD:]

            chosen = jnp.concatenate(
                [
                    jnp.broadcast_to(
                        jnp.where(low == 0, here[i : i + 1, :], here[i + 2 : i + 3, :]), (128, 128)
                    ).T
                    for i in range(2)
                ],
                axis=0,
            )
            cross = jnp.zeros((half, L), jnp.float32)
            for p in range(NPROMPT):
                one = lax.dot_general(
                    qv, pk[p][...], (((1,), (1,)), ((), ())),
                    preferred_element_type=jnp.float32,
                )
                cross = jnp.where(chosen == float(p), one, cross)
            cross_top = jnp.max(cross, axis=1, keepdims=True)
            weights = jnp.exp2((cross - cross_top) * SCALE)
            total = jnp.sum(weights, axis=1, keepdims=True)
            masked = jnp.concatenate(
                [
                    jnp.where(chosen == float(p), weights, 0.0).astype(jnp.bfloat16)
                    for p in range(NPROMPT)
                ],
                axis=1,
            )
            stacked = jnp.concatenate([pkv[p, 1] for p in range(NPROMPT)], axis=0)
            result = result + jnp.dot(
                masked, stacked, preferred_element_type=jnp.float32
            ) / total
            ob[pl.ds(row, half), :] = (gate * result).astype(jnp.bfloat16)

            target = base + s + 1
            for i in range(nz // 2):
                z2 = low * (nz // 2) + i
                src = ob.at[pl.ds(pl.multiple_of(row + i * rows, rows), rows), :]
                dst = out.at[:, pl.ds(head_col, HD)]
                mine = (target == q) & (j == z2)

                @pl.when(mine)
                def _():
                    pltpu.make_async_copy(src, dst, out_sem).start()

                @pl.when(jnp.logical_not(mine) & (target < nq))
                def _():
                    pltpu.make_async_remote_copy(
                        src_ref=src, dst_ref=dst, send_sem=out_send, recv_sem=out_sem,
                        device_id={"queue": target, "head": z2}, device_id_type=MESH,
                    ).start()

            return carry

        lax.fori_loop(0, 2 * GROUP, one_block, 0)
        for side in range(2):

            @pl.when(sides[side][0])
            def _():
                wait_for(kv.at[:, :slab, :], halo_send.at[side])

        for slabs, there in ((GROUP, has_right), (GROUP - 1, jnp.logical_not(has_right))):

            @pl.when(there & (a == 0))
            def _():
                wait_for(ob.at[: slabs * slab, :], out_send)

            @pl.when(there & (a > 0))
            def _():
                wait_for(ob.at[: slabs * slab - rows, :], out_send)

    @pl.when(jnp.logical_not(works))
    def _():
        wait_for(meta, meta_sem)
        prompt_copy.wait()

    if not THROTTLE:
        sent(1, 3, kv_send)
    sent(0, 1, q_send)
    for i in range(GROUP - 1):
        wait_for(meta_src, meta_send.at[i])

    @pl.when(q > 0)
    def _():
        wait_for(out, out_sem)


def solution(mesh):
    nq, nz = mesh.shape["queue"], mesh.shape["head"]

    def per_device(
        projected, prompt_states, region_map, region_prompt, step_index, time_gates, incoming
    ):
        rows, _, channels = projected.shape
        slab = rows * nz
        anywhere = pl.BlockSpec(memory_space=pl.ANY)
        scalars = pl.BlockSpec(memory_space=pltpu.SMEM)
        dma = pltpu.SemaphoreType.DMA

        def kernel(*refs):
            attention_kernel(nq, nz, *refs)

        moved = pl.pallas_call(
            kernel,
            out_shape=jax.ShapeDtypeStruct((rows, channels), jnp.bfloat16),
            in_specs=[anywhere, anywhere, anywhere, scalars, scalars, anywhere],
            out_specs=anywhere,
            scratch_shapes=[
                pltpu.VMEM((2, (GROUP + 2) * slab, HD), jnp.bfloat16),
                pltpu.VMEM((1, GROUP * slab, HD), jnp.bfloat16),
                pltpu.VMEM((GROUP * slab, HD), jnp.bfloat16),
                pltpu.VMEM((NPROMPT, 2, L, HD), jnp.bfloat16),
                pltpu.VMEM(region_map.shape, jnp.int32),
                pltpu.VMEM(time_gates.shape, jnp.float32),
                pltpu.VMEM((8, 128), jnp.float32),
                pltpu.VMEM((GROUP, 8, 128), jnp.float32),
                dma((GROUP, nz)),
                pltpu.SemaphoreType.REGULAR((3,)),
                dma((2 * GROUP,)),
                dma((2,)),
                dma,
                dma,
                dma((3,)),
                dma,
                dma,
                dma((2,)),
                dma((GROUP - 1,)),
                dma,
            ],
            compiler_params=pltpu.CompilerParams(
                collective_id=0, has_side_effects=True, vmem_limit_bytes=63_400_000
            ),
        )(
            projected.transpose(1, 0, 2), prompt_states, region_map, region_prompt, step_index,
            time_gates,
        )
        return jnp.where(lax.axis_index("queue") == 0, incoming, moved)

    return jax.shard_map(
        per_device,
        mesh=mesh,
        in_specs=(
            P(("queue", "head"), None, None),
            P(None, None, None, "head"),
            P("queue", None),
            P("queue", None),
            P("queue"),
            P(None, "head"),
            P("head", None),
        ),
        out_specs=P(("queue", "head"), None),
        check_vma=False,
    )
```

```python
import math

import jax
import jax.numpy as jnp
from jax import lax
from jax.experimental import pallas as pl
from jax.experimental.pallas import tpu as pltpu
from jax.sharding import PartitionSpec as P

HD = 128
L = 128
R = 4
NPROMPT = 8
GROUP = 4
PER = 3

NEG = -1e30
FAR = 1e30
SCALE = math.log2(math.e) / math.sqrt(HD)
THROTTLE = False
MESH = pl.DeviceIdType.MESH


def free_place(z):
    upper = (z == 1) | (z == 3) | (z == 4) | (z == 7)
    return jnp.where(upper, 3, 1)


def wrapped(value, count):
    return jnp.where(value >= count, value - count, jnp.where(value < 0, value + count, value))


def wait_for(ref, sem):
    pltpu.make_async_copy(ref, ref, sem).wait()


def attention_kernel(
    nq, nz,
    proj, prompts, rmap, rprompt, step, gates,
    out,
    kv, qb, ob, pkv, rmap_v, gates_v, meta_src, meta,
    kv_sem, ready, q_sem, halo_sem, meta_sem, out_sem, local_sem,
    kv_send, q_send, halo_send, meta_send, out_send,
):
    rows = proj.shape[1]
    slab = rows * nz
    half = slab // 2
    heads = PER * nz
    ring = 2 * nz
    q = lax.axis_index("queue")
    j = lax.axis_index("head")
    c = lax.div(q, GROUP)
    base = c * GROUP
    a = q - base
    arc = jnp.where(a >= 2, 1, 0)
    core = a - 2 * arc
    z = arc * nz + j
    free = free_place(j)
    works = a != free
    hl = a - jnp.where(a > free, 1, 0)
    has_left = c > 0
    has_right = q + GROUP < nq
    sides = ((has_left, q - GROUP), (has_right, q + GROUP))

    barrier = pltpu.get_barrier_semaphore()

    def greet(chip, k):
        upper = jnp.where(chip >= nz, 1, 0)
        pl.semaphore_signal(
            barrier, inc=1,
            device_id={"queue": base + 2 * upper + k, "head": chip - nz * upper},
            device_id_type=MESH,
        )

    for off in (1, -1):
        chip = wrapped(z + off, ring)
        greet(chip, 0)
        greet(chip, 1)
    greet(z, 1 - core)
    for there, other in sides:

        @pl.when(there)
        def _():
            pl.semaphore_signal(
                barrier, inc=1, device_id={"queue": other, "head": j}, device_id_type=MESH
            )

    map_copy = pltpu.make_async_copy(rmap, rmap_v, local_sem.at[0])
    gate_copy = pltpu.make_async_copy(gates, gates_v, local_sem.at[1])
    lane = pl.multiple_of(jnp.minimum(hl, PER - 1) * HD, HD)
    prompt_copy = pltpu.make_async_copy(
        prompts.at[:, :, :, pl.ds(lane, HD)], pkv, local_sem.at[2]
    )
    map_copy.start()
    gate_copy.start()
    prompt_copy.start()
    both_sides = has_left & has_right

    @pl.when(both_sides)
    def _():
        pl.semaphore_wait(barrier, 7)

    @pl.when(jnp.logical_not(both_sides))
    def _():
        pl.semaphore_wait(barrier, 6)

    for there, slot in ((has_left, 0), (has_right, GROUP + 1)):

        @pl.when(jnp.logical_not(there))
        def _():
            kv[:, slot * slab : (slot + 1) * slab, :] = jnp.zeros((2, slab, HD), jnp.bfloat16)


    def tell(n):
        for off in (2**n, -(2**n)):
            chip = wrapped(z + off, ring)
            upper = jnp.where(chip >= nz, 1, 0)
            pl.semaphore_signal(
                ready.at[n], inc=1,
                device_id={"queue": base + 2 * upper + core, "head": chip - nz * upper},
                device_id_type=MESH,
            )

    rounds = nz.bit_length() - 1
    tell(0)

    def spread(first, last, dst, send_sem, recv_sem, opening):
        def piece(chip, k):
            upper = jnp.where(chip >= nz, 1, 0)
            z2 = chip - nz * upper
            a2 = 2 * upper + k
            free2 = free_place(z2)
            hl2 = a2 - jnp.where(a2 > free2, 1, 0)
            col = pl.multiple_of((z2 * PER + jnp.minimum(hl2, PER - 1)) * HD, HD)
            return a2 != free2, base + a2, z2, proj.at[first:last, :, pl.ds(col, HD)]

        def send(chip, k):
            real, q2, z2, src = piece(chip, k)

            def go():
                pltpu.make_async_remote_copy(
                    src_ref=src, dst_ref=dst, send_sem=send_sem, recv_sem=recv_sem,
                    device_id={"queue": q2, "head": z2}, device_id_type=MESH,
                ).start()

            if k == 0:
                go()
            else:
                pl.when(real)(go)

        def both_ways(m, carry):
            for off in (m, -m):
                chip = wrapped(z + off, ring)
                send(chip, 0)
                send(chip, 1)
            return carry

        @pl.when(works)
        def _():
            pltpu.make_async_copy(piece(z, core)[3], dst, recv_sem).start()

        for k in range(2):
            @pl.when((core != k) & ((k == 0) | (2 * arc + 1 != free)))
            def _():
                real, q2, z2, src = piece(z, k)
                pltpu.make_async_remote_copy(
                    src_ref=src, dst_ref=dst, send_sem=send_sem, recv_sem=recv_sem,
                    device_id={"queue": q2, "head": z2}, device_id_type=MESH,
                ).start()

        if opening:
            for n in range(rounds):
                lax.fori_loop(2**n // 2 + 1, 2**n + 1, both_ways, 0)
                pl.semaphore_wait(ready.at[n], 2)
                if n + 1 < rounds:
                    tell(n + 1)
            lax.fori_loop(nz // 2 + 1, nz, both_ways, 0)
        else:
            lax.fori_loop(1, nz, lambda m, carry: both_ways(nz - m, carry), 0)
        opposite = wrapped(z + nz, ring)
        send(opposite, 0)
        send(opposite, 1)

    def sent(first, last, sem):
        @pl.when(works)
        def _():
            wait_for(proj.at[first:last, :, : (heads - 1) * HD], sem)

        @pl.when(jnp.logical_not(works))
        def _():
            wait_for(proj.at[first:last], sem)

    kv_row = pl.multiple_of((a + 1) * slab + j * rows, rows)
    kv_dst = kv.at[:, pl.ds(kv_row, rows), :]
    spread(1, 3, kv_dst, kv_send, kv_sem.at[a, j], True)

    map_copy.wait()
    gate_copy.wait()
    regions = rmap_v[...]
    token_prompt = jnp.zeros(regions.shape, jnp.int32)
    for r in range(R):
        token_prompt = jnp.where(regions == r, rprompt[0, r], token_prompt)
    token_prompt = token_prompt.astype(jnp.float32)
    for i in range(slab // 128):
        meta_src[i : i + 1, :] = token_prompt[:, i * 128 : (i + 1) * 128]
    table = gates_v[...]
    picked = lax.broadcasted_iota(jnp.int32, table.shape, 0) == step[0]
    gate_row = jnp.sum(jnp.where(picked, table, 0.0), axis=0, keepdims=True)
    for i in range(PER):
        meta_src[4 + i : 5 + i, :] = gate_row[:, i * HD : (i + 1) * HD]
    meta_src[7:8, :] = jnp.zeros((1, 128), jnp.float32)
    pltpu.make_async_copy(meta_src, meta.at[a], meta_sem).start()
    for i in range(1, GROUP):
        pltpu.make_async_remote_copy(
            src_ref=meta_src, dst_ref=meta.at[a], send_sem=meta_send.at[i - 1], recv_sem=meta_sem,
            device_id={"queue": base + wrapped(a + i, GROUP), "head": j},
            device_id_type=MESH,
        ).start()

    if THROTTLE:
        sent(1, 3, kv_send)
    q_row = pl.multiple_of(a * slab + j * rows, rows)
    spread(
        0, 1, qb.at[:, pl.ds(q_row, rows), :], q_send,
        q_sem.at[a * 2 + jnp.where(j >= nz // 2, 1, 0)], False,
    )

    @pl.when(works)
    def _():
        def halo(side, n):
            src, dst, to = ((1, GROUP + 1, q - GROUP), (GROUP, 0, q + GROUP))[side]
            return pltpu.make_async_remote_copy(
                src_ref=kv.at[:, pl.ds(pl.multiple_of(src * slab + n * rows, rows), rows), :],
                dst_ref=kv.at[:, pl.ds(pl.multiple_of(dst * slab + n * rows, rows), rows), :],
                send_sem=halo_send.at[side], recv_sem=halo_sem.at[side],
                device_id={"queue": to, "head": j}, device_id_type=MESH,
            )

        def forward(n, carry):
            for side in range(2):
                src = (1, GROUP)[side]
                wait_for(
                    kv.at[:, pl.ds(pl.multiple_of(src * slab + n * rows, rows), rows), :],
                    kv_sem.at[src - 1, n],
                )


                @pl.when(sides[side][0])
                def _():
                    halo(side, n).start()

            for s in range(1, GROUP - 1):
                wait_for(
                    kv.at[:, pl.ds(pl.multiple_of((s + 1) * slab + n * rows, rows), rows), :],
                    kv_sem.at[s, n],
                )
            return carry

        lax.fori_loop(0, nz, forward, 0)
        wait_for(meta, meta_sem)
        prompt_copy.wait()
        head_col = pl.multiple_of((j * PER + hl) * HD, HD)
        pk = [pkv.at[p, 0] for p in range(NPROMPT)]
        ones = jnp.ones((3 * slab, HD), jnp.bfloat16)
        within = jnp.where(j >= nz // 2, j - nz // 2, j)
        mine4 = 2 * arc + jnp.where(j >= nz // 2, 1, 0)

        def one_block(t, carry):
            turn = jnp.where(t >= 6, 3, jnp.where(t >= 4, 2, jnp.where(t >= 2, 1, 0)))
            targets = (
                jnp.where(mine4 == 0, 0, jnp.where(mine4 == 1, 3, jnp.where(mine4 == 2, 0, 0))),
                jnp.where(mine4 == 0, 2, jnp.where(mine4 == 1, 0, jnp.where(mine4 == 2, 3, 2))),
                jnp.where(mine4 == 0, 3, jnp.where(mine4 == 1, 2, jnp.where(mine4 == 2, 1, 1))),
                jnp.where(mine4 == 0, 1, jnp.where(mine4 == 1, 1, jnp.where(mine4 == 2, 2, 3))),
            )
            quarter = jnp.where(turn == 0, targets[0], jnp.where(turn == 1, targets[1], jnp.where(turn == 2, targets[2], targets[3])))
            side = jnp.where(quarter >= 2, 1, 0)
            low = quarter - 2 * side
            s = wrapped(2 * side + t - 2 * turn - 1, GROUP)

            @pl.when(t == 0)
            def _():
                @pl.when(has_right)
                def _():
                    wait_for(kv.at[:, (GROUP + 1) * slab :, :], halo_sem.at[0])

                @pl.when(has_left)
                def _():
                    wait_for(kv.at[:, :slab, :], halo_sem.at[1])


            left_ok = has_left | (s > 0)
            right_ok = has_right | (s < GROUP - 1)
            here = meta[s]
            gate = jnp.where(
                hl == 0, here[4:5, :], jnp.where(hl == 1, here[5:6, :], here[6:7, :])
            )
            row = pl.multiple_of(s * slab + low * half, half)
            wait_for(qb.at[:, pl.ds(row, half), :], q_sem.at[s * 2 + low])
            qv = qb[0, pl.ds(row, half), :]
            first = pl.multiple_of(s * slab, slab)
            keys = kv[0, pl.ds(first, 3 * slab), :]
            values = kv[1, pl.ds(first, 3 * slab), :]
            scores = lax.dot_general(
                qv, keys, (((1,), (1,)), ((), ())), preferred_element_type=jnp.float32
            )
            parts = [scores[:, i * slab : (i + 1) * slab] for i in range(3)]
            tops = [jnp.max(x, axis=1, keepdims=True) for x in parts]
            top = jnp.maximum(
                tops[1],
                jnp.maximum(jnp.where(left_ok, tops[0], NEG), jnp.where(right_ok, tops[2], NEG)),
            )
            shifts = (jnp.where(left_ok, top, FAR), top, jnp.where(right_ok, top, FAR))
            probs = jnp.concatenate(
                [jnp.exp2((x - y) * SCALE).astype(jnp.bfloat16) for x, y in zip(parts, shifts)],
                axis=1,
            )
            both = jnp.dot(
                probs, jnp.concatenate([values, ones], axis=1),
                preferred_element_type=jnp.float32,
            )
            result = both[:, :HD] / both[:, HD:]

            chosen = jnp.concatenate(
                [
                    jnp.broadcast_to(
                        jnp.where(low == 0, here[i : i + 1, :], here[i + 2 : i + 3, :]), (128, 128)
                    ).T
                    for i in range(2)
                ],
                axis=0,
            )
            cross = jnp.zeros((half, L), jnp.float32)
            for p in range(NPROMPT):
                one = lax.dot_general(
                    qv, pk[p][...], (((1,), (1,)), ((), ())),
                    preferred_element_type=jnp.float32,
                )
                cross = jnp.where(chosen == float(p), one, cross)
            cross_top = jnp.max(cross, axis=1, keepdims=True)
            weights = jnp.exp2((cross - cross_top) * SCALE)
            total = jnp.sum(weights, axis=1, keepdims=True)
            masked = jnp.concatenate(
                [
                    jnp.where(chosen == float(p), weights, 0.0).astype(jnp.bfloat16)
                    for p in range(NPROMPT)
                ],
                axis=1,
            )
            stacked = jnp.concatenate([pkv[p, 1] for p in range(NPROMPT)], axis=0)
            result = result + jnp.dot(
                masked, stacked, preferred_element_type=jnp.float32
            ) / total
            ob[pl.ds(row, half), :] = (gate * result).astype(jnp.bfloat16)

            target = base + s + 1
            for i in range(nz // 2):
                z2 = low * (nz // 2) + i
                src = ob.at[pl.ds(pl.multiple_of(row + i * rows, rows), rows), :]
                dst = out.at[:, pl.ds(head_col, HD)]
                mine = (target == q) & (j == z2)

                @pl.when(mine)
                def _():
                    pltpu.make_async_copy(src, dst, out_sem).start()

                @pl.when(jnp.logical_not(mine) & (target < nq))
                def _():
                    pltpu.make_async_remote_copy(
                        src_ref=src, dst_ref=dst, send_sem=out_send, recv_sem=out_sem,
                        device_id={"queue": target, "head": z2}, device_id_type=MESH,
                    ).start()

            return carry

        lax.fori_loop(0, 2 * GROUP, one_block, 0)
        for side in range(2):

            @pl.when(sides[side][0])
            def _():
                wait_for(kv.at[:, :slab, :], halo_send.at[side])

        for slabs, there in ((GROUP, has_right), (GROUP - 1, jnp.logical_not(has_right))):

            @pl.when(there & (a == 0))
            def _():
                wait_for(ob.at[: slabs * slab, :], out_send)

            @pl.when(there & (a > 0))
            def _():
                wait_for(ob.at[: slabs * slab - rows, :], out_send)

    @pl.when(jnp.logical_not(works))
    def _():
        wait_for(meta, meta_sem)
        prompt_copy.wait()

    if not THROTTLE:
        sent(1, 3, kv_send)
    sent(0, 1, q_send)
    for i in range(GROUP - 1):
        wait_for(meta_src, meta_send.at[i])

    @pl.when(q > 0)
    def _():
        wait_for(out, out_sem)


def solution(mesh):
    nq, nz = mesh.shape["queue"], mesh.shape["head"]

    def per_device(
        projected, prompt_states, region_map, region_prompt, step_index, time_gates, incoming
    ):
        rows, _, channels = projected.shape
        slab = rows * nz
        anywhere = pl.BlockSpec(memory_space=pl.ANY)
        scalars = pl.BlockSpec(memory_space=pltpu.SMEM)
        dma = pltpu.SemaphoreType.DMA

        def kernel(*refs):
            attention_kernel(nq, nz, *refs)

        moved = pl.pallas_call(
            kernel,
            out_shape=jax.ShapeDtypeStruct((rows, channels), jnp.bfloat16),
            in_specs=[anywhere, anywhere, anywhere, scalars, scalars, anywhere],
            out_specs=anywhere,
            scratch_shapes=[
                pltpu.VMEM((2, (GROUP + 2) * slab, HD), jnp.bfloat16),
                pltpu.VMEM((1, GROUP * slab, HD), jnp.bfloat16),
                pltpu.VMEM((GROUP * slab, HD), jnp.bfloat16),
                pltpu.VMEM((NPROMPT, 2, L, HD), jnp.bfloat16),
                pltpu.VMEM(region_map.shape, jnp.int32),
                pltpu.VMEM(time_gates.shape, jnp.float32),
                pltpu.VMEM((8, 128), jnp.float32),
                pltpu.VMEM((GROUP, 8, 128), jnp.float32),
                dma((GROUP, nz)),
                pltpu.SemaphoreType.REGULAR((3,)),
                dma((2 * GROUP,)),
                dma((2,)),
                dma,
                dma,
                dma((3,)),
                dma,
                dma,
                dma((2,)),
                dma((GROUP - 1,)),
                dma,
            ],
            compiler_params=pltpu.CompilerParams(
                collective_id=0, has_side_effects=True, vmem_limit_bytes=63_400_000
            ),
        )(
            projected.transpose(1, 0, 2), prompt_states, region_map, region_prompt, step_index,
            time_gates,
        )
        return jnp.where(lax.axis_index("queue") == 0, incoming, moved)

    return jax.shard_map(
        per_device,
        mesh=mesh,
        in_specs=(
            P(("queue", "head"), None, None),
            P(None, None, None, "head"),
            P("queue", None),
            P("queue", None),
            P("queue"),
            P(None, "head"),
            P("head", None),
        ),
        out_specs=P(("queue", "head"), None),
        check_vma=False,
    )
```
